512 devices in a mesh: fsdp: 32 (over z, y_hi, core), expert: 16 (over x, y_lo).
Axes of the slice: x: 4, y: 8 (y_hi: 2, y_lo: 4; y = y_hi * 4 + y_lo), z: 8, core: 2. Of those that a mesh axis runs over, the one named last changes fastest.
Arguments:
- latent: bfloat16 [65536, 512], P(('fsdp', 'expert')), may hold values from -6 to 6
- routes: int32 [65536, 2], P(('fsdp', 'expert')), may hold values from 0 to 15, all different within a row; in each aligned block of 128 rows (0 to 127, 128 to 255, ...) at most 32 rows name the same one
- scores: float32 [65536, 2], P(('fsdp', 'expert')), may hold values from 0.2 to 1
- cotangent: bfloat16 [65536, 512], P(('fsdp', 'expert')), may hold values from -6 to 6
- w_gate: bfloat16 [16, 1344, 512], P('expert', 'fsdp'), may hold values from -0.25 to 0.25
- w_up: bfloat16 [16, 1344, 512], P('expert', 'fsdp'), may hold values from -0.25 to 0.25
- w_down: bfloat16 [16, 1344, 512], P('expert', 'fsdp'), may hold values from -0.15625 to 0.15625
Outputs:
- mixed: bfloat16 [65536, 512], P(('fsdp', 'expert'))
- latent_grad: bfloat16 [65536, 512], P(('fsdp', 'expert'))
- score_grad: float32 [65536, 2], P(('fsdp', 'expert'))
- gate_grad: float32 [16, 1344, 512], P('expert', 'fsdp')
- up_grad: float32 [16, 1344, 512], P('expert', 'fsdp')
- down_grad: float32 [16, 1344, 512], P('expert', 'fsdp')
The draws below stay inside these ranges and needn't reach their ends.
Inputs may be any that keep to these rules, and one draw needn't show every extreme that they name: `routes`: each row names two different experts. Among the 128 rows of one device no expert is named more than 32 times; in some device's rows some expert is named exactly 32 times.
All inputs are finite; a program needn't handle non-finite values.
Results may differ from the reference program's by a relative error of at most 0.023.
Values may be sent and summed in bfloat16 or wider, within the bound.
No kernel may reach another device: no remote copies, remote signals or barrier semaphores. Data moves between devices by JAX's collectives and lax.ppermute only.
A program may use at most 64 MiB of HBM per device.

```python
import math
import jax
import jax.numpy as jnp
import numpy as np
from jax import lax

C = 512
H = 1344
TOK_DEV = 128
EXPERTS = 16
CAP = 32
TOKENS = 65536
N_FSDP = 32
N_EXPERT = 16


def levels(key, shape, cuts, low, largest):
    def one(position, blocks):
        heights = jax.random.uniform(jax.random.fold_in(jax.random.fold_in(key, 6), position), (blocks,), jnp.float32, low / len(cuts), largest / len(cuts))
        return jnp.repeat(jnp.exp(heights), shape[position] // blocks).reshape((-1,) + (1,) * (len(shape) - position - 1))

    loudness = one(*cuts[0])
    for cut in cuts[1:]:
        loudness = loudness * one(*cut)
    return loudness


def assign_block(own_key, own, number, rows, count, top, bound, slope):
    ranking = jax.random.permutation(own_key, count)
    heavy_load, usual = shares(count, rows * top, bound, slope, True), shares(count, rows * top, bound, slope, False)
    places = jnp.arange(count)

    def named(sizes, turn):
        used = int((sizes > 0).sum())
        fixed = max(1, used // 4)
        shifted = fixed + (places - fixed + turn * (used - fixed)) % max(1, count - fixed)
        return jnp.zeros((count,), jnp.int32).at[ranking[jnp.where(places < fixed, places, shifted)]].set(jnp.asarray(sizes, jnp.int32))

    sizes = jnp.where(number % 4 == 0, named(heavy_load, number // 4), named(usual, number - number // 4 - 1))
    mixed = jax.random.permutation(jax.random.fold_in(own, 3), count)
    source_of, sink = mixed[0:count // 2 * 2:2], mixed[1:count // 2 * 2:2]
    margin = jnp.minimum(sizes[source_of] - 1, bound - sizes[sink]) // 2
    margin = jnp.where((source_of == ranking[0]) | (sink == ranking[0]) | (sizes[sink] == 0), 0, jnp.maximum(margin, 0))
    shifted = jax.random.randint(jax.random.fold_in(own, 4), (count // 2,), 0, 1 << 20) % (margin + 1)
    sizes = sizes.at[source_of].add(-shifted).at[sink].add(shifted)
    labels = jnp.searchsorted(jnp.cumsum(sizes), jnp.arange(rows * top), side="right").astype(jnp.int32)
    listing = labels.reshape(top, rows).T
    listing = listing[jax.random.permutation(jax.random.fold_in(own, 1), rows)]
    turn = jax.random.randint(jax.random.fold_in(own, 2), (rows, 1), 0, top)
    return jnp.take_along_axis(listing, (jnp.arange(top)[None, :] + turn) % top, axis=1)


def shares(amount, total, bound, skew, full):
    loads = [(1 << 20) // math.isqrt(rank ** skew) + 1 for rank in range(1, amount + 1)]
    largest = bound if full else min(bound, max(-(-total // amount), total * loads[0] // sum(loads)))
    least = 1 if total - largest >= amount - 1 else 0
    given, spare = [largest] + [least] * (amount - 1), total - largest - least * (amount - 1)
    while spare > 0:
        candidates = [i for i in range(1, amount) if given[i] < largest] or [i for i in range(1, amount) if given[i] < bound]
        pool, left = sum([loads[i] for i in candidates]), spare
        for i in candidates:
            addition = min(bound - given[i], max(1, left * loads[i] // pool), spare)
            given[i] = given[i] + addition
            spare = spare - addition
    return np.array(given)


def bell_draw(key, extent, scale, bound, pieces=(), kind=jnp.bfloat16):
    result = jax.random.normal(key, extent, jnp.float32) * scale
    if len(pieces) > 0:
        result = levels(key, extent, pieces, -0.22, 0.18) * result
    return jnp.clip(result, min=-bound, max=bound).astype(kind)


def setup_inputs(seed: int = 0) -> dict:
    keys = jax.random.split(jax.random.key(seed), 8)
    latent = bell_draw(keys[0], (TOKENS, C), 1.0, 6.0, ((0, 512),))
    routes_keys = jax.random.split(jax.random.fold_in(keys[1], 1), TOKENS // TOK_DEV)
    routes_turns = jax.random.permutation(jax.random.fold_in(keys[1], 3), TOKENS // TOK_DEV)
    routes = jax.vmap(lambda own, number: assign_block(jax.random.fold_in(keys[1], 2), own, number, TOK_DEV, EXPERTS, 2, CAP, 1))(routes_keys, routes_turns).reshape((TOKENS, 2))
    scores = jnp.clip(0.2 + 0.8 * jax.random.uniform(keys[2], (TOKENS, 2), jnp.float32) ** levels(keys[2], (TOKENS, 2), ((0, 512),), -0.2, 0.2), 0.2, 1.0)
    cotangent = bell_draw(keys[3], (TOKENS, C), 1.0, 6.0, ((0, 512),))
    w_gate = bell_draw(keys[4], (EXPERTS, H, C), C ** -0.5, 0.25, ((0, 16), (1, 32)))
    w_up = bell_draw(keys[5], (EXPERTS, H, C), C ** -0.5, 0.25, ((0, 16), (1, 32)))
    w_down = bell_draw(keys[6], (EXPERTS, H, C), H ** -0.5, 0.15625, ((0, 16), (1, 32)))
    return {"latent": latent, "routes": routes, "scores": scores, "cotangent": cotangent, "w_gate": w_gate, "w_up": w_up, "w_down": w_down}


grad_scale = 0.015625


def silu_parts(gate):
    sig = jax.nn.sigmoid(gate)
    return gate * sig, sig * (1.0 + gate * (1.0 - sig))


def group_partial(left, right, width):
    left_f = left.reshape(N_FSDP, -1, left.shape[-1]).astype(jnp.float32)
    right_f = right.reshape(N_FSDP, -1, width).astype(jnp.float32)
    partial_sums = jnp.einsum("grh,grc->ghc", left_f, right_f) * grad_scale
    rounded = lax.optimization_barrier(partial_sums.astype(jnp.bfloat16))
    return jnp.sum(rounded.astype(jnp.float32), axis=0)


def take_rows(source, index):
    return jax.vmap(lambda block, rows: block[rows])(source, index)


def reference(latent, routes, scores, cotangent, w_gate, w_up, w_down):
    devices = N_FSDP * N_EXPERT
    width = latent.shape[1]
    picks = 2 * TOK_DEV
    tokens = latent.reshape(devices, TOK_DEV, width)
    cots = cotangent.reshape(devices, TOK_DEV, width)
    chosen = routes.reshape(devices, picks).astype(jnp.int32)
    weights = scores.reshape(devices, picks)
    expert_ids = jnp.arange(EXPERTS, dtype=jnp.int32)
    onehot = (chosen[:, :, None] == expert_ids[None, None, :]).astype(jnp.int32)
    ranks = jnp.sum((jnp.cumsum(onehot, axis=1) - 1) * onehot, axis=2).astype(jnp.int32)
    slots = (chosen * CAP + ranks).astype(jnp.int32)
    device_ids = jnp.broadcast_to(jnp.arange(devices, dtype=jnp.int32)[:, None], (devices, picks))
    pick_ids = jnp.broadcast_to(jnp.arange(picks, dtype=jnp.int32)[None, :], (devices, picks))
    table = jnp.full((devices, EXPERTS * CAP), picks, jnp.int32).at[device_ids, slots].set(pick_ids)
    table = table.reshape(devices, EXPERTS, CAP).transpose(1, 0, 2)

    def step(carry, inputs):
        mixed_acc, back_acc, score_acc = carry
        picked, wg, wu, wd = inputs
        valid = picked < picks
        safe = jnp.where(valid, picked, 0).astype(jnp.int32)
        tok_index = (safe // 2).astype(jnp.int32)
        rows = take_rows(tokens, tok_index)
        rows = jnp.where(valid[:, :, None], rows, jnp.zeros((), jnp.bfloat16))
        cot_rows = take_rows(cots, tok_index).astype(jnp.float32)
        pick_weight = jnp.where(valid, jnp.take_along_axis(weights, safe, axis=1), jnp.float32(0.0))
        flat = rows.reshape(-1, width)
        gate = lax.dot_general(flat, wg, (((1,), (1,)), ((), ())), preferred_element_type=jnp.float32)
        up = lax.dot_general(flat, wu, (((1,), (1,)), ((), ())), preferred_element_type=jnp.float32)
        act, deriv = silu_parts(gate)
        hidden = (act * up).astype(jnp.bfloat16)
        outs = jnp.dot(hidden, wd, preferred_element_type=jnp.float32).astype(jnp.bfloat16)
        outs_f = outs.reshape(devices, CAP, width).astype(jnp.float32)
        out_grad = (pick_weight[:, :, None] * cot_rows).astype(jnp.bfloat16).reshape(-1, width)
        hidden_grad = lax.dot_general(out_grad, wd, (((1,), (1,)), ((), ())), preferred_element_type=jnp.float32)
        gate_back = (hidden_grad * up * deriv).astype(jnp.bfloat16)
        up_back = (hidden_grad * act).astype(jnp.bfloat16)
        token_back = (jnp.dot(gate_back, wg, preferred_element_type=jnp.float32)
                      + jnp.dot(up_back, wu, preferred_element_type=jnp.float32)).astype(jnp.bfloat16)
        gate_grad = group_partial(gate_back, flat, width)
        up_grad = group_partial(up_back, flat, width)
        down_grad = group_partial(hidden, out_grad, width)
        tok_drop = jnp.where(valid, tok_index, TOK_DEV).astype(jnp.int32)
        pick_drop = jnp.where(valid, picked, picks).astype(jnp.int32)
        contrib = pick_weight[:, :, None] * outs_f
        mixed_acc = jax.vmap(lambda acc, i, v: acc.at[i].add(v, mode="drop"))(mixed_acc, tok_drop, contrib)
        back_f = token_back.reshape(devices, CAP, width).astype(jnp.float32)
        back_acc = jax.vmap(lambda acc, i, v: acc.at[i].add(v, mode="drop"))(back_acc, tok_drop, back_f)
        inner = jnp.sum(cot_rows * outs_f, axis=2)
        score_acc = jax.vmap(lambda acc, i, v: acc.at[i].set(v, mode="drop"))(score_acc, pick_drop, inner)
        return (mixed_acc, back_acc, score_acc), (gate_grad, up_grad, down_grad)

    start = (jnp.zeros((devices, TOK_DEV, width), jnp.float32),
             jnp.zeros((devices, TOK_DEV, width), jnp.float32),
             jnp.zeros((devices, picks), jnp.float32))
    (mixed_acc, back_acc, score_acc), grads = lax.scan(step, start, (table, w_gate, w_up, w_down))
    mixed = mixed_acc.reshape(-1, width).astype(jnp.bfloat16)
    latent_grad = back_acc.reshape(-1, width).astype(jnp.bfloat16)
    score_grad = score_acc.reshape(-1, 2)
    return (mixed, latent_grad, score_grad, grads[0], grads[1], grads[2])
```

```python
import jax
import jax.numpy as jnp
from jax import lax
from jax.sharding import Mesh, PartitionSpec as P

grad_scale = 0.015625
PAD = 48
F32 = jnp.float32
BF16 = jnp.bfloat16


def partner_pairs(rounds, size):
    pairs = []
    for z in range(size):
        for core in range(2):
            odd_link = (rounds + core) % 2
            step = 1 if (z + odd_link) % 2 == 0 else -1
            pairs.append((z * 2 + core, (z + step) % size * 2 + core))
    return pairs


def swap_z(rows, rounds):
    size = lax.axis_size("z")
    return lax.ppermute(rows, ("z", "core"), partner_pairs(rounds, size))


def swap(rows, axis):
    return lax.ppermute(rows, axis, [(0, 1), (1, 0)])


def gather_z(block):
    got = swap_z(block, 0)
    pieces = [jnp.concatenate([block, got], axis=0)]
    for rounds in (1, 2, 3):
        pieces.append(swap_z(pieces[-1], rounds))
    return pieces


def add(one, two):
    return one.astype(F32) + two.astype(F32)


def sum_z(pieces):
    first, second, third, last = pieces
    third = add(third, swap_z(last, 3)).astype(BF16)
    second = add(second, swap_z(third, 2)).astype(BF16)
    first = add(first, swap_z(second, 1))
    return add(first[:1], swap_z(first[1:].astype(BF16), 0))


def against(left, right):
    return lax.dot_general(left, right, (((1,), (1,)), ((), ())), preferred_element_type=F32)


def outer_sum(left, right):
    return lax.dot_general(left, right, (((0,), (0,)), ((), ())), preferred_element_type=F32)


def slot_tables(routes, experts, capacity):
    rows = routes.shape[0]
    ids = jnp.arange(experts, dtype=jnp.int32)[None, :]
    named = ((routes[:, 0:1] == ids) | (routes[:, 1:2] == ids)).astype(BF16)
    earlier = (
        jnp.arange(rows)[:, None] > jnp.arange(rows)[None, :]
    ).astype(BF16)
    ranks = jnp.dot(earlier, named, preferred_element_type=F32)
    slots = ids.astype(F32) * capacity + ranks
    slot = [
        jnp.sum(jnp.where(routes[:, k : k + 1] == ids, slots, 0.0), axis=1, keepdims=True)
        for k in range(2)
    ]
    positions = jnp.arange(experts * capacity, dtype=jnp.int32).astype(F32)[None, :]
    return [s == positions for s in slot]


def shards(latent, routes, scores, cotangent, w_gate, w_up, w_down):
    experts = lax.axis_size("x") * lax.axis_size("yl")
    tok_rows, width = latent.shape
    capacity = 4 * tok_rows // experts
    slots = experts * capacity
    hidden_rows = w_gate.shape[1]
    own = jnp.pad(
        jnp.stack([w_gate[0], w_up[0], w_down[0]]), ((0, 0), (0, PAD - hidden_rows), (0, 0))
    )[None]
    other = swap(own, "yh")

    first, second = slot_tables(routes, experts, capacity)
    first_b, second_b = first.astype(BF16), second.astype(BF16)
    merged = first_b + second_b
    score_slot = jnp.sum(
        jnp.where(first, scores[:, 0:1], 0.0) + jnp.where(second, scores[:, 1:2], 0.0), axis=0
    )[:, None]
    send = outer_sum(merged, latent).astype(BF16)
    grad_send = (outer_sum(merged, cotangent) * score_slot).astype(BF16)
    shape = (experts, capacity, width)
    both = jnp.concatenate([send.reshape(shape), grad_send.reshape(shape)], axis=1)
    mine = lax.all_to_all(both, ("x", "yl"), 0, 0, tiled=True)
    theirs = swap(mine, "core")

    pieces = gather_z(own) + gather_z(other)
    weights = jnp.concatenate(pieces, axis=0)
    blocks = weights.shape[0]
    wg, wu, wd = [weights[:, i].reshape(blocks * PAD, width) for i in range(3)]

    def tokens(part):
        rows = slice(part * capacity, (part + 1) * capacity)
        return jnp.concatenate(
            [mine[:, rows].reshape(slots, width), theirs[:, rows].reshape(slots, width)], axis=0
        )

    arrived, out_grad = tokens(0), tokens(1)
    gate = against(arrived, wg)
    up = against(arrived, wu)
    sig = jax.nn.sigmoid(gate)
    act = gate * sig
    hidden = (act * up).astype(BF16)
    outs = jnp.dot(hidden, wd, preferred_element_type=F32)
    hidden_grad = against(out_grad, wd)
    gate_back = (hidden_grad * up * sig * (1.0 + gate * (1.0 - sig))).astype(BF16)
    up_back = (hidden_grad * act).astype(BF16)
    token_back = jnp.dot(gate_back, wg, preferred_element_type=F32) + jnp.dot(
        up_back, wu, preferred_element_type=F32
    )
    terms = jnp.stack(
        [
            (outer_sum(left, right) * grad_scale).astype(BF16).reshape(blocks, PAD, width)
            for left, right in ((gate_back, arrived), (up_back, arrived), (hidden, out_grad))
        ],
        axis=1,
    )
    quarter = blocks // 8
    parts = [terms[i * quarter : (i + 1) * quarter] for i in range(8)]
    far = sum_z(parts[4:]).astype(BF16)
    near = sum_z(parts[:4])
    grads = add(near, swap(far, "yh"))[0, :, :hidden_rows]

    rest = swap(
        jnp.concatenate(
            [outs[slots:].reshape(shape), token_back[slots:].reshape(shape)], axis=1
        ).astype(BF16),
        "core",
    )
    local = jnp.concatenate(
        [outs[:slots].reshape(shape), token_back[:slots].reshape(shape)], axis=1
    )
    back = lax.all_to_all(add(local, rest).astype(BF16), ("x", "yl"), 0, 0, tiled=True)
    outs_back = back[:, :capacity].reshape(slots, width)
    tokens_back = back[:, capacity:].reshape(slots, width)
    out_first = jnp.dot(first_b, outs_back, preferred_element_type=F32)
    out_second = jnp.dot(second_b, outs_back, preferred_element_type=F32)
    mixed = (scores[:, 0:1] * out_first + scores[:, 1:2] * out_second).astype(BF16)
    cot_f = cotangent.astype(F32)
    score_grad = jnp.stack(
        [jnp.sum(cot_f * out_first, axis=1), jnp.sum(cot_f * out_second, axis=1)], axis=1
    )
    latent_grad = jnp.dot(merged, tokens_back, preferred_element_type=F32).astype(BF16)
    return (mixed, latent_grad, score_grad, grads[0:1], grads[1:2], grads[2:3])


def solution(mesh):
    fine = Mesh(
        mesh.devices.reshape(8, 2, 2, 4, 4), ("z", "yh", "core", "x", "yl")
    )
    fsdp, expert = ("z", "yh", "core"), ("x", "yl")
    rows = P(fsdp + expert, None)
    weight = P(expert, fsdp, None)
    return jax.shard_map(
        shards,
        mesh=fine,
        in_specs=(rows,) * 4 + (weight,) * 3,
        out_specs=(rows,) * 3 + (weight,) * 3,
        check_vma=False,
    )
```

```python
import functools

import jax
import jax.numpy as jnp
from jax import lax
from jax.experimental import pallas as pl
from jax.experimental.pallas import tpu as pltpu
from jax.sharding import Mesh, PartitionSpec as P

grad_scale = 0.015625
PAD = 48
F32 = jnp.float32
BF16 = jnp.bfloat16


def swap_z(rows, parity):
    size = lax.axis_size("z")
    pairs = [(z, (z + (1 if (z + parity) % 2 == 0 else -1)) % size) for z in range(size)]
    return lax.ppermute(rows, "z", pairs)


def swap(rows, axis):
    return lax.ppermute(rows, axis, [(0, 1), (1, 0)])


def add(one, two):
    return one.astype(F32) + two.astype(F32)


together = lax.optimization_barrier


def sum_z(pieces, parity):
    first, second, third, last = pieces
    third = add(third, swap_z(last, parity + 3)).astype(BF16)
    second = add(second, swap_z(third, parity + 2)).astype(BF16)
    first = add(first, swap_z(second, parity + 1))
    return add(first[:1], swap_z(first[1:].astype(BF16), parity))


def dot(left, right, contract):
    return lax.dot_general(left, right, ((contract[:1], contract[1:]), ((), ())), preferred_element_type=F32)


def kernel_call(body, outs, scratch=(), flops=0, grant=32):
    return pl.pallas_call(
        body,
        out_shape=outs,
        scratch_shapes=list(scratch),
        compiler_params=pltpu.CompilerParams(vmem_limit_bytes=grant * 2**20),
        cost_estimate=pl.CostEstimate(flops=flops, bytes_accessed=1 << 20, transcendentals=0),
    )


def dispatch_body(capacity, latent, cotangent, routes, scores, send, first, second):
    experts = send.shape[0]
    slots, rows = first.shape
    width = latent.shape[1]
    slot = lax.broadcasted_iota(jnp.int32, (slots, rows), 0)
    bits = capacity.bit_length() - 1
    expert = slot >> bits
    place = slot & (capacity - 1)
    named_0 = routes[0:1, :] == expert
    named_1 = routes[1:2, :] == expert
    named = jnp.where(named_0 | named_1, 1.0, 0.0)
    upper = lax.broadcasted_iota(jnp.int32, (rows, rows), 0) < lax.broadcasted_iota(
        jnp.int32, (rows, rows), 1
    )
    ranks = dot(named.astype(BF16), jnp.where(upper, 1.0, 0.0).astype(BF16), (1, 0))
    hit = ranks == place.astype(F32)
    one = jnp.where(named_0 & hit, 1.0, 0.0)
    two = jnp.where(named_1 & hit, 1.0, 0.0)
    first[...] = one.astype(BF16)
    second[...] = two.astype(BF16)
    table = (one + two).astype(BF16)
    score = jnp.sum(one * scores[0:1, :] + two * scores[1:2, :], axis=1, keepdims=True)
    placed = dot(table, latent[...], (1, 0)).astype(BF16)
    weighted = (score * dot(table, cotangent[...], (1, 0))).astype(BF16)
    send[:, :capacity, :] = placed.reshape(experts, capacity, width)
    send[:, capacity:, :] = weighted.reshape(experts, capacity, width)


def combine_body(capacity, back, first, second, scores, cotangent, mixed, latent_grad, score_grad):
    slots, rows = first.shape
    width = back.shape[2]
    outs = back[:, :capacity, :].reshape(slots, width)
    tokens = back[:, capacity:, :].reshape(slots, width)
    cot = cotangent[...].astype(F32)
    total = jnp.zeros((rows, width), F32)
    sums = []
    for k, table in enumerate((first, second)):
        picked = dot(table[...], outs, (0, 0))
        score = jnp.broadcast_to(scores[k : k + 1, :], (rows, rows)).T
        total = total + score[:, 0:1] * picked
        own = jnp.sum(cot * picked, axis=1, keepdims=True)
        sums.append(jnp.broadcast_to(own, (rows, rows)).T[0:1, :])
    mixed[...] = total.astype(BF16)
    score_grad[...] = jnp.concatenate(sums, axis=0)
    merged = first[...] + second[...]
    latent_grad[...] = dot(merged, tokens, (0, 0)).astype(BF16)


def expert_body(capacity, last, *refs):
    mine, theirs = refs[:2]
    pieces = refs[2:6]
    refs = refs[6:]
    if last:
        sums, refs = refs[:2], refs[2:]
    grads = refs[:4]
    results = refs[4:6]
    wg, wu, wd, xs, gs, hs, gbs, ubs = refs[6:]
    width = mine.shape[2]
    for i, piece in enumerate(pieces):
        for j in range(2):
            block = slice((2 * i + j) * PAD, (2 * i + j + 1) * PAD)
            for k, weight in enumerate((wg, wu, wd)):
                weight[block, :] = piece[j, k]
    sources = mine.shape[0] // 2
    tile = sources * capacity
    for i in range(4):
        tokens = (mine, theirs)[i // 2]
        part = slice((i % 2) * sources, (i % 2 + 1) * sources)
        rows = slice(i * tile, (i + 1) * tile)
        x = tokens[part, :capacity, :].reshape(tile, width)
        g = tokens[part, capacity:, :].reshape(tile, width)
        xs[rows, :] = x
        gs[rows, :] = g
        gate = dot(x, wg[...], (1, 1))
        up = dot(x, wu[...], (1, 1))
        hidden_grad = dot(g, wd[...], (1, 1))
        sig = jax.nn.sigmoid(gate)
        act = gate * sig
        hidden = (act * up).astype(BF16)
        gate_back = (hidden_grad * up * (sig * (1.0 + gate * (1.0 - sig)))).astype(BF16)
        up_back = (hidden_grad * act).astype(BF16)
        hs[rows, :] = hidden
        gbs[rows, :] = gate_back
        ubs[rows, :] = up_back
        outs = dot(hidden, wd[...], (1, 0)).reshape(sources, capacity, width)
        back = dot(gate_back, wg[...], (1, 0)) + dot(up_back, wu[...], (1, 0))
        back = back.reshape(sources, capacity, width)
        result = results[i // 2]
        if last:
            outs = outs + sums[i // 2][part, :capacity, :]
            back = back + sums[i // 2][part, capacity:, :]
        result[part, :capacity, :] = outs.astype(result.dtype)
        result[part, capacity:, :] = back.astype(result.dtype)
    for k, (left, right) in enumerate(((gbs, xs), (ubs, xs), (hs, gs))):
        term = (dot(left[...], right[...], (0, 0)) * grad_scale).astype(BF16)
        for i, grad in enumerate(grads):
            for j in range(2):
                grad[j, k] = term[(2 * i + j) * PAD : (2 * i + j + 1) * PAD, :]


def expert_call(capacity, mine, theirs, pieces, sums=()):
    last = len(sums) > 0
    both = mine.shape
    width = both[2]
    slots = both[0] * capacity * 2
    hidden = 8 * PAD
    outs = [jax.ShapeDtypeStruct(p.shape, BF16) for p in pieces]
    outs += [jax.ShapeDtypeStruct(both, F32), jax.ShapeDtypeStruct(both, BF16 if last else F32)]
    scratch = [pltpu.VMEM((hidden, width), BF16)] * 3 + [pltpu.VMEM((slots, width), BF16)] * 2
    scratch += [pltpu.VMEM((slots, hidden), BF16)] * 3
    call = kernel_call(
        functools.partial(expert_body, capacity, last), outs, scratch, 18 * slots * hidden * width
    )
    got = call(mine, theirs, *pieces, *sums)
    return got[:4], got[4:]


def shards(latent, routes, scores, cotangent, w_gate, w_up, w_down):
    experts = lax.axis_size("x") * lax.axis_size("yl")
    tok_rows, width = latent.shape
    capacity = 4 * tok_rows // experts
    slots = experts * capacity
    hidden_rows = w_gate.shape[1]
    own = jnp.pad(
        jnp.stack([w_gate[0], w_up[0], w_down[0]]), ((0, 0), (0, PAD - hidden_rows), (0, 0))
    )[None]
    other = swap(own, "yh")

    shape = (experts, 2 * capacity, width)
    table = jax.ShapeDtypeStruct((slots, tok_rows), BF16)
    score_rows = scores.T
    send, first, second = kernel_call(
        functools.partial(dispatch_body, capacity),
        [jax.ShapeDtypeStruct(shape, BF16), table, table],
        grant=56,
    )(latent, cotangent, routes.T, score_rows)

    near_got = swap_z(own, 0)
    other, near_got, send = together((other, near_got, send))
    mine = lax.all_to_all(send, ("x", "yl"), 0, 0, tiled=True)
    near = [jnp.concatenate([own, near_got], axis=0)]
    near.append(swap_z(near[0], 1))
    far_got = swap_z(other, 0)
    near[1], far_got = together((near[1], far_got))
    far = [jnp.concatenate([other, far_got], axis=0)]
    near.append(swap_z(near[1], 0))
    far.append(swap_z(far[0], 1))
    near[2], far[1], mine = together((near[2], far[1], mine))
    near.append(swap_z(near[2], 1))
    far.append(swap_z(far[1], 0))
    theirs = swap(mine, "core")
    near[3], far[2], theirs = together((near[3], far[2], theirs))
    far.append(swap_z(far[2], 1))

    near_terms, sums = expert_call(capacity, mine, theirs, near)
    far_terms, (local, rest) = expert_call(capacity, mine, theirs, far, sums)

    far_sum = sum_z(far_terms, 0).astype(BF16)
    near_sum = sum_z(near_terms, 0)
    back = lax.all_to_all(
        add(local, swap(rest, "core")).astype(BF16), ("x", "yl"), 0, 0, tiled=True
    )
    got = swap(far_sum, "yh")
    row = jax.ShapeDtypeStruct((tok_rows, width), BF16)
    mixed, latent_grad, score_grad = kernel_call(
        functools.partial(combine_body, capacity),
        [row, row, jax.ShapeDtypeStruct((2, tok_rows), F32)],
    )(back, first, second, score_rows, cotangent)
    got, mixed = together((got, mixed))
    grads = (near_sum + got.astype(F32))[0, :, :hidden_rows]
    return (mixed, latent_grad, score_grad.T, grads[0:1], grads[1:2], grads[2:3])


def solution(mesh):
    fine = Mesh(
        mesh.devices.reshape(8, 2, 2, 4, 4), ("z", "yh", "core", "x", "yl")
    )
    fsdp, expert = ("z", "yh", "core"), ("x", "yl")
    rows = P(fsdp + expert, None)
    weight = P(expert, fsdp, None)
    return jax.shard_map(
        shards,
        mesh=fine,
        in_specs=(rows,) * 4 + (weight,) * 3,
        out_specs=(rows,) * 3 + (weight,) * 3,
        check_vma=False,
    )
```

```python
import functools

import jax
import jax.numpy as jnp
from jax import lax
from jax.experimental import pallas as pl
from jax.experimental.pallas import tpu as pltpu
from jax.sharding import Mesh, PartitionSpec as P

grad_scale = 0.015625
PAD = 48
F32 = jnp.float32
BF16 = jnp.bfloat16


def swap_z(rows, parity):
    size = lax.axis_size("z")
    pairs = [(z, (z + (1 if (z + parity) % 2 == 0 else -1)) % size) for z in range(size)]
    return lax.ppermute(rows, "z", pairs)


def swap(rows, axis):
    return lax.ppermute(rows, axis, [(0, 1), (1, 0)])


def add(one, two):
    return one.astype(F32) + two.astype(F32)


together = lax.optimization_barrier


def sum_z(pieces, parity):
    first, second, third, last = pieces
    third = add(third, swap_z(last, parity + 3)).astype(BF16)
    second = add(second, swap_z(third, parity + 2)).astype(BF16)
    first = add(first, swap_z(second, parity + 1))
    return add(first[:1], swap_z(first[1:].astype(BF16), parity))


def dot(left, right, contract):
    return lax.dot_general(left, right, ((contract[:1], contract[1:]), ((), ())), preferred_element_type=F32)


def kernel_call(body, outs, scratch=(), flops=0, grant=32):
    return pl.pallas_call(
        body,
        out_shape=outs,
        scratch_shapes=list(scratch),
        compiler_params=pltpu.CompilerParams(vmem_limit_bytes=grant * 2**20),
        cost_estimate=pl.CostEstimate(flops=flops, bytes_accessed=1 << 20, transcendentals=0),
    )


def dispatch_body(capacity, latent, cotangent, routes, scores, send, first, second):
    experts = send.shape[0]
    slots, rows = first.shape
    width = latent.shape[1]
    slot = lax.broadcasted_iota(jnp.int32, (slots, rows), 0)
    bits = capacity.bit_length() - 1
    expert = slot >> bits
    place = slot & (capacity - 1)
    named_0 = routes[0:1, :] == expert
    named_1 = routes[1:2, :] == expert
    named = jnp.where(named_0 | named_1, 1.0, 0.0)
    upper = lax.broadcasted_iota(jnp.int32, (rows, rows), 0) < lax.broadcasted_iota(
        jnp.int32, (rows, rows), 1
    )
    ranks = dot(named.astype(BF16), jnp.where(upper, 1.0, 0.0).astype(BF16), (1, 0))
    hit = ranks == place.astype(F32)
    one = jnp.where(named_0 & hit, 1.0, 0.0)
    two = jnp.where(named_1 & hit, 1.0, 0.0)
    first[...] = one.astype(BF16)
    second[...] = two.astype(BF16)
    table = (one + two).astype(BF16)
    score = jnp.sum(one * scores[0:1, :] + two * scores[1:2, :], axis=1, keepdims=True)
    placed = dot(table, latent[...], (1, 0)).astype(BF16)
    weighted = (score * dot(table, cotangent[...], (1, 0))).astype(BF16)
    send[:, :capacity, :] = placed.reshape(experts, capacity, width)
    send[:, capacity:, :] = weighted.reshape(experts, capacity, width)


def combine_body(capacity, back, first, second, scores, cotangent, mixed, latent_grad, score_grad):
    slots, rows = first.shape
    width = back.shape[2]
    outs = back[:, :capacity, :].reshape(slots, width)
    tokens = back[:, capacity:, :].reshape(slots, width)
    cot = cotangent[...].astype(F32)
    total = jnp.zeros((rows, width), F32)
    sums = []
    for k, table in enumerate((first, second)):
        picked = dot(table[...], outs, (0, 0))
        score = jnp.broadcast_to(scores[k : k + 1, :], (rows, rows)).T
        total = total + score[:, 0:1] * picked
        own = jnp.sum(cot * picked, axis=1, keepdims=True)
        sums.append(jnp.broadcast_to(own, (rows, rows)).T[0:1, :])
    mixed[...] = total.astype(BF16)
    score_grad[...] = jnp.concatenate(sums, axis=0)
    merged = first[...] + second[...]
    latent_grad[...] = dot(merged, tokens, (0, 0)).astype(BF16)


def expert_body(capacity, count, more, *refs):
    mine, theirs = refs[:2]
    pieces = refs[2 : 2 + count]
    refs = refs[2 + count :]
    if more:
        sums, refs = refs[:2], refs[2:]
    grads = refs[:count]
    results = refs[count : count + 2]
    wg, wu, wd, xs, gs, hs, gbs, ubs = refs[count + 2 :]
    width = mine.shape[2]
    own_rows = pieces[0].shape[1] // 3
    for i, piece in enumerate(pieces):
        for j in range(2):
            start = (2 * i + j) * PAD
            for k, weight in enumerate((wg, wu, wd)):
                weight[start : start + own_rows, :] = piece[j, k * own_rows : (k + 1) * own_rows, :]
                weight[start + own_rows : start + PAD, :] = jnp.zeros((PAD - own_rows, width), BF16)
    sources = mine.shape[0] // 2
    tile = sources * capacity
    for i in range(4):
        tokens = (mine, theirs)[i // 2]
        part = slice((i % 2) * sources, (i % 2 + 1) * sources)
        rows = slice(i * tile, (i + 1) * tile)
        x = tokens[part, :capacity, :].reshape(tile, width)
        g = tokens[part, capacity:, :].reshape(tile, width)
        xs[rows, :] = x
        gs[rows, :] = g
        gate = dot(x, wg[...], (1, 1))
        up = dot(x, wu[...], (1, 1))
        hidden_grad = dot(g, wd[...], (1, 1))
        sig = jax.nn.sigmoid(gate)
        act = gate * sig
        hidden = (act * up).astype(BF16)
        gate_back = (hidden_grad * up * (sig * (1.0 + gate * (1.0 - sig)))).astype(BF16)
        up_back = (hidden_grad * act).astype(BF16)
        hs[rows, :] = hidden
        gbs[rows, :] = gate_back
        ubs[rows, :] = up_back
        outs = dot(hidden, wd[...], (1, 0)).reshape(sources, capacity, width)
        back = dot(gate_back, wg[...], (1, 0)) + dot(up_back, wu[...], (1, 0))
        back = back.reshape(sources, capacity, width)
        result = results[i // 2]
        if more:
            outs = outs + sums[i // 2][part, :capacity, :]
            back = back + sums[i // 2][part, capacity:, :]
        result[part, :capacity, :] = outs.astype(result.dtype)
        result[part, capacity:, :] = back.astype(result.dtype)
    for k, (left, right) in enumerate(((gbs, xs), (ubs, xs), (hs, gs))):
        term = (dot(left[...], right[...], (0, 0)) * grad_scale).astype(BF16)
        for i, grad in enumerate(grads):
            for j in range(2):
                start = (2 * i + j) * PAD
                grad[j, k * own_rows : (k + 1) * own_rows, :] = term[start : start + own_rows, :]


def expert_call(capacity, mine, theirs, pieces, sums=(), last=False):
    both = mine.shape
    width = both[2]
    slots = both[0] * capacity * 2
    count = len(pieces)
    hidden = 2 * count * PAD
    outs = [jax.ShapeDtypeStruct(p.shape, BF16) for p in pieces]
    outs += [jax.ShapeDtypeStruct(both, F32), jax.ShapeDtypeStruct(both, BF16 if last else F32)]
    scratch = [pltpu.VMEM((hidden, width), BF16)] * 3 + [pltpu.VMEM((slots, width), BF16)] * 2
    scratch += [pltpu.VMEM((slots, hidden), BF16)] * 3
    body = functools.partial(expert_body, capacity, count, len(sums) > 0)
    call = kernel_call(body, outs, scratch, 18 * slots * hidden * width)
    got = call(mine, theirs, *pieces, *sums)
    return got[:count], got[count:]


def pair_body(one, two, out):
    out[0:1] = one[...]
    out[1:2] = two[...]


def pair(one, two, flops=0):
    out = jax.ShapeDtypeStruct((2,) + one.shape[1:], one.dtype)
    return kernel_call(pair_body, out, flops=flops, grant=16)(one, two)


def total_body(one, two, out):
    out[...] = (one[...].astype(F32) + two[...].astype(F32)).astype(out.dtype)


def total(one, two, dtype, flops=0):
    out = jax.ShapeDtypeStruct(one.shape, dtype)
    return kernel_call(total_body, out, flops=flops, grant=16)(one, two)


def finish_body(near, far, *outs):
    value = near[0] + far[0].astype(F32)
    rows = value.shape[0] // 3
    for k, out in enumerate(outs):
        for j in range(value.shape[1] // 128):
            out[pl.ds(j, rows, stride=value.shape[1] // 128), :] = value[
                k * rows : (k + 1) * rows, j * 128 : (j + 1) * 128
            ]


def shards(latent, routes, scores, cotangent, w_gate, w_up, w_down):
    experts = lax.axis_size("x") * lax.axis_size("yl")
    tok_rows, width = latent.shape
    capacity = 4 * tok_rows // experts
    slots = experts * capacity
    hidden_rows = w_gate.shape[1]
    own = jnp.concatenate([w_gate[0], w_up[0], w_down[0]], axis=0)[None]
    other = swap(own, "yh")

    near_got = swap_z(own, 0)
    shape = (experts, 2 * capacity, width)
    table = jax.ShapeDtypeStruct((slots, tok_rows), BF16)
    score_rows = scores.T
    send, first, second = kernel_call(
        functools.partial(dispatch_body, capacity),
        [jax.ShapeDtypeStruct(shape, BF16), table, table],
        grant=56,
    )(latent, cotangent, routes.T, score_rows)

    other, near_got, send = together((other, near_got, send))
    mine = lax.all_to_all(send, ("x", "yl"), 0, 0, tiled=True)
    near = [jnp.concatenate([own, near_got], axis=0)]
    near.append(swap_z(near[0], 1))
    far_got = swap_z(other, 0)
    near[1], far_got = together((near[1], far_got))
    far = [pair(other, far_got, 4 * 10**10)]
    near.append(swap_z(near[1], 0))
    far.append(swap_z(far[0], 1))
    near[2], far[1] = together((near[2], far[1]))
    near.append(swap_z(near[2], 1))
    far.append(swap_z(far[1], 0))
    near[3], far[2], mine = together((near[3], far[2], mine))
    theirs = swap(mine, "core")
    far.append(swap_z(far[2], 1))

    near_terms, sums = expert_call(capacity, mine, theirs, near)
    early, sums = expert_call(capacity, mine, theirs, far[:3], sums)
    late, (local, rest) = expert_call(capacity, mine, theirs, far[3:], sums, True)
    far_terms = (*early, *late)

    near_got = swap_z(near_terms[3], 1)
    rest = swap(rest, "core")
    near_sum = add(near_terms[2], near_got).astype(BF16)
    near_got, got, rest = together((swap_z(near_sum, 0), swap_z(far_terms[3], 1), rest))
    far_sum = add(far_terms[2], got).astype(BF16)
    near_sum = add(near_terms[1], near_got).astype(BF16)
    back = lax.all_to_all(add(local, rest).astype(BF16), ("x", "yl"), 0, 0, tiled=True)
    near_got, got = together((swap_z(near_sum, 1), swap_z(far_sum, 0)))
    far_sum = total(far_terms[1], got, BF16, 4 * 10**10)
    near_sum = add(near_terms[0], near_got)
    near_got, got = together((swap_z(near_sum[1:].astype(BF16), 0), swap_z(far_sum, 1)))
    near_sum = add(near_sum[:1], near_got)
    far_sum = add(far_terms[0], got)
    far_sum = add(far_sum[:1], swap_z(far_sum[1:].astype(BF16), 0)).astype(BF16)
    got = swap(far_sum, "yh")
    row = jax.ShapeDtypeStruct((tok_rows, width), BF16)
    mixed, latent_grad, score_grad = kernel_call(
        functools.partial(combine_body, capacity),
        [row, row, jax.ShapeDtypeStruct((2, tok_rows), F32)],
    )(back, first, second, score_rows, cotangent)
    got, mixed = together((got, mixed))
    lanes = width // 128
    block = jax.ShapeDtypeStruct((hidden_rows * lanes, 128), F32)
    grads = kernel_call(finish_body, [block] * 3)(near_sum, got)
    grads = [grad.reshape(1, hidden_rows, width) for grad in grads]
    return (mixed, latent_grad, score_grad.T, *grads)


def solution(mesh):
    fine = Mesh(
        mesh.devices.reshape(8, 2, 2, 4, 4), ("z", "yh", "core", "x", "yl")
    )
    fsdp, expert = ("z", "yh", "core"), ("x", "yl")
    rows = P(fsdp + expert, None)
    weight = P(expert, fsdp, None)
    return jax.shard_map(
        shards,
        mesh=fine,
        in_specs=(rows,) * 4 + (weight,) * 3,
        out_specs=(rows,) * 3 + (weight,) * 3,
        check_vma=False,
    )
```

```python
import functools

import jax
import jax.numpy as jnp
from jax import lax
from jax.experimental import pallas as pl
from jax.experimental.pallas import tpu as pltpu
from jax.sharding import Mesh, PartitionSpec as P

grad_scale = 0.015625
PAD = 48
F32 = jnp.float32
BF16 = jnp.bfloat16


def swap_z(rows, parity):
    size = lax.axis_size("z")
    pairs = [(z, (z + (1 if (z + parity) % 2 == 0 else -1)) % size) for z in range(size)]
    return lax.ppermute(rows, "z", pairs)


def swap(rows, axis):
    return lax.ppermute(rows, axis, [(0, 1), (1, 0)])


def add(one, two):
    return one.astype(F32) + two.astype(F32)


together = lax.optimization_barrier


def sum_z(pieces, parity):
    first, second, third, last = pieces
    third = add(third, swap_z(last, parity + 3)).astype(BF16)
    second = add(second, swap_z(third, parity + 2)).astype(BF16)
    first = add(first, swap_z(second, parity + 1))
    return add(first[:1], swap_z(first[1:].astype(BF16), parity))


def dot(left, right, contract):
    return lax.dot_general(left, right, ((contract[:1], contract[1:]), ((), ())), preferred_element_type=F32)


def kernel_call(body, outs, scratch=(), flops=0, grant=24):
    return pl.pallas_call(
        body,
        out_shape=outs,
        scratch_shapes=list(scratch),
        compiler_params=pltpu.CompilerParams(vmem_limit_bytes=grant * 2**20),
        cost_estimate=pl.CostEstimate(flops=flops, bytes_accessed=1 << 20, transcendentals=0),
    )


def dispatch_body(capacity, latent, cotangent, routes, scores, send, first, second):
    experts = send.shape[0]
    slots, rows = first.shape
    width = latent.shape[1]
    slot = lax.broadcasted_iota(jnp.int32, (slots, rows), 0)
    bits = capacity.bit_length() - 1
    expert = slot >> bits
    place = slot & (capacity - 1)
    named_0 = routes[0:1, :] == expert
    named_1 = routes[1:2, :] == expert
    named = jnp.where(named_0 | named_1, 1.0, 0.0)
    upper = lax.broadcasted_iota(jnp.int32, (rows, rows), 0) < lax.broadcasted_iota(
        jnp.int32, (rows, rows), 1
    )
    ranks = dot(named.astype(BF16), jnp.where(upper, 1.0, 0.0).astype(BF16), (1, 0))
    hit = ranks == place.astype(F32)
    one = jnp.where(named_0 & hit, 1.0, 0.0)
    two = jnp.where(named_1 & hit, 1.0, 0.0)
    first[...] = one.astype(BF16)
    second[...] = two.astype(BF16)
    table = (one + two).astype(BF16)
    score = jnp.sum(one * scores[0:1, :] + two * scores[1:2, :], axis=1, keepdims=True)
    placed = dot(table, latent[...], (1, 0)).astype(BF16)
    weighted = (score * dot(table, cotangent[...], (1, 0))).astype(BF16)
    send[:, :capacity, :] = placed.reshape(experts, capacity, width)
    send[:, capacity:, :] = weighted.reshape(experts, capacity, width)


def combine_body(capacity, back, first, second, scores, cotangent, mixed, latent_grad, score_grad):
    slots, rows = first.shape
    width = back.shape[2]
    outs = back[:, :capacity, :].reshape(slots, width)
    tokens = back[:, capacity:, :].reshape(slots, width)
    cot = cotangent[...].astype(F32)
    total = jnp.zeros((rows, width), F32)
    sums = []
    for k, table in enumerate((first, second)):
        picked = dot(table[...], outs, (0, 0))
        score = jnp.broadcast_to(scores[k : k + 1, :], (rows, rows)).T
        total = total + score[:, 0:1] * picked
        own = jnp.sum(cot * picked, axis=1, keepdims=True)
        sums.append(jnp.broadcast_to(own, (rows, rows)).T[0:1, :])
    mixed[...] = total.astype(BF16)
    score_grad[...] = jnp.concatenate(sums, axis=0)
    merged = first[...] + second[...]
    latent_grad[...] = dot(merged, tokens, (0, 0)).astype(BF16)


def expert_body(capacity, count, more, *refs):
    mine, theirs = refs[:2]
    pieces = refs[2 : 2 + count]
    refs = refs[2 + count :]
    if more:
        sums, refs = refs[:2], refs[2:]
    grads = refs[:count]
    results = refs[count : count + 2]
    wg, wu, wd, xs, gs, hs, gbs, ubs = refs[count + 2 :]
    width = mine.shape[2]
    own_rows = pieces[0].shape[1] // 3
    for i, piece in enumerate(pieces):
        for j in range(2):
            start = (2 * i + j) * PAD
            for k, weight in enumerate((wg, wu, wd)):
                weight[start : start + own_rows, :] = piece[j, k * own_rows : (k + 1) * own_rows, :]
                weight[start + own_rows : start + PAD, :] = jnp.zeros((PAD - own_rows, width), BF16)
    sources = mine.shape[0] // 2
    tile = sources * capacity
    for i in range(4):
        tokens = (mine, theirs)[i // 2]
        part = slice((i % 2) * sources, (i % 2 + 1) * sources)
        rows = slice(i * tile, (i + 1) * tile)
        x = tokens[part, :capacity, :].reshape(tile, width)
        g = tokens[part, capacity:, :].reshape(tile, width)
        xs[rows, :] = x
        gs[rows, :] = g
        gate = dot(x, wg[...], (1, 1))
        up = dot(x, wu[...], (1, 1))
        hidden_grad = dot(g, wd[...], (1, 1))
        sig = jax.nn.sigmoid(gate)
        act = gate * sig
        hidden = (act * up).astype(BF16)
        gate_back = (hidden_grad * up * (sig * (1.0 + gate * (1.0 - sig)))).astype(BF16)
        up_back = (hidden_grad * act).astype(BF16)
        hs[rows, :] = hidden
        gbs[rows, :] = gate_back
        ubs[rows, :] = up_back
        outs = dot(hidden, wd[...], (1, 0)).reshape(sources, capacity, width)
        back = dot(gate_back, wg[...], (1, 0)) + dot(up_back, wu[...], (1, 0))
        back = back.reshape(sources, capacity, width)
        result = results[i // 2]
        if more:
            outs = outs + sums[i // 2][part, :capacity, :]
            back = back + sums[i // 2][part, capacity:, :]
        result[part, :capacity, :] = outs.astype(result.dtype)
        result[part, capacity:, :] = back.astype(result.dtype)
    for k, (left, right) in enumerate(((gbs, xs), (ubs, xs), (hs, gs))):
        term = (dot(left[...], right[...], (0, 0)) * grad_scale).astype(BF16)
        for i, grad in enumerate(grads):
            for j in range(2):
                start = (2 * i + j) * PAD
                grad[j, k * own_rows : (k + 1) * own_rows, :] = term[start : start + own_rows, :]


def expert_call(capacity, mine, theirs, pieces, sums=(), last=False):
    both = mine.shape
    width = both[2]
    slots = both[0] * capacity * 2
    count = len(pieces)
    hidden = 2 * count * PAD
    outs = [jax.ShapeDtypeStruct(p.shape, BF16) for p in pieces]
    outs += [jax.ShapeDtypeStruct(both, F32), jax.ShapeDtypeStruct(both, BF16 if last else F32)]
    scratch = [pltpu.VMEM((hidden, width), BF16)] * 3 + [pltpu.VMEM((slots, width), BF16)] * 2
    scratch += [pltpu.VMEM((slots, hidden), BF16)] * 3
    body = functools.partial(expert_body, capacity, count, len(sums) > 0)
    call = kernel_call(body, outs, scratch, 18 * slots * hidden * width)
    got = call(mine, theirs, *pieces, *sums)
    return got[:count], got[count:]


def pair_body(one, two, out):
    out[0:1] = one[...]
    out[1:2] = two[...]


def pair(one, two, flops=0):
    out = jax.ShapeDtypeStruct((2,) + one.shape[1:], one.dtype)
    return kernel_call(pair_body, out, flops=flops, grant=16)(one, two)


def total_body(one, two, out):
    out[...] = (one[...].astype(F32) + two[...].astype(F32)).astype(out.dtype)


def total(one, two, dtype, flops=0):
    out = jax.ShapeDtypeStruct(one.shape, dtype)
    return kernel_call(total_body, out, flops=flops, grant=16)(one, two)


def split_body(one, two, keep, send):
    value = one[...].astype(F32) + two[...].astype(F32)
    keep[...] = value[0:1]
    send[...] = value[1:2].astype(send.dtype)


def split(one, two, flops=0):
    shape = (1,) + one.shape[1:]
    outs = [jax.ShapeDtypeStruct(shape, F32), jax.ShapeDtypeStruct(shape, BF16)]
    return kernel_call(split_body, outs, flops=flops, grant=16)(one, two)


def finish_body(near, near_far, far, *outs):
    value = near[0] + near_far[0].astype(F32) + far[0].astype(F32)
    rows = value.shape[0] // 3
    for k, out in enumerate(outs):
        for j in range(value.shape[1] // 128):
            out[pl.ds(j, rows, stride=value.shape[1] // 128), :] = value[
                k * rows : (k + 1) * rows, j * 128 : (j + 1) * 128
            ]


def shards(latent, routes, scores, cotangent, w_gate, w_up, w_down):
    experts = lax.axis_size("x") * lax.axis_size("yl")
    tok_rows, width = latent.shape
    capacity = 4 * tok_rows // experts
    slots = experts * capacity
    hidden_rows = w_gate.shape[1]
    own = jnp.concatenate([w_gate[0], w_up[0], w_down[0]], axis=0)[None]
    other = swap(own, "yh")

    near_got = swap_z(own, 0)
    shape = (experts, 2 * capacity, width)
    table = jax.ShapeDtypeStruct((slots, tok_rows), BF16)
    score_rows = scores.T
    send, first, second = kernel_call(
        functools.partial(dispatch_body, capacity),
        [jax.ShapeDtypeStruct(shape, BF16), table, table],
        grant=56,
    )(latent, cotangent, routes.T, score_rows)

    other, near_got, send = together((other, near_got, send))
    mine = lax.all_to_all(send, ("x", "yl"), 0, 0, tiled=True)
    near = [jnp.concatenate([own, near_got], axis=0)]
    far_got = swap_z(other, 0)
    near.append(swap_z(near[0], 1))
    far = [pair(other, far_got, 4 * 10**10)]
    near.append(swap_z(near[1], 0))
    far.append(swap_z(far[0], 1))
    near[2], far[1] = together((near[2], far[1]))
    near.append(swap_z(near[2], 1))
    far.append(swap_z(far[1], 0))
    near[3], far[2], mine = together((near[3], far[2], mine))
    theirs = swap(mine, "core")
    far.append(swap_z(far[2], 1))

    near_terms, sums = expert_call(capacity, mine, theirs, near)
    early, sums = expert_call(capacity, mine, theirs, far[:3], sums)
    late, (local, rest) = expert_call(capacity, mine, theirs, far[3:], sums, True)
    far_terms = (*early, *late)

    rest = swap(rest, "core")
    got = swap_z(far_terms[3], 1)
    far_sum = total(far_terms[2], got, BF16, 4 * 10**10)
    far_sum, rest = together((far_sum, rest))
    back = lax.all_to_all(add(local, rest).astype(BF16), ("x", "yl"), 0, 0, tiled=True)
    got, near_got = together((swap_z(far_sum, 0), swap_z(near_terms[3], 1)))
    far_sum = total(far_terms[1], got, BF16, 0)
    far_sum, near_got = together((far_sum, near_got))
    near_sum = total(near_terms[2], near_got, BF16, 4 * 10**9)
    got, near_got = together((swap_z(far_sum, 1), swap_z(near_sum, 0)))
    far_keep, far_send = split(far_terms[0], got)
    far_send, near_got = together((far_send, near_got))
    near_sum = total(near_terms[1], near_got, BF16, 4 * 10**9)
    got, near_got = together((swap_z(far_send, 0), swap_z(near_sum, 1)))
    far_sum = total(far_keep, got, BF16)
    far_sum, near_got = together((far_sum, near_got))
    near_keep, near_send = split(near_terms[0], near_got, 4 * 10**9)
    near_got = swap_z(near_send, 0)
    got = swap(far_sum, "yh")
    row = jax.ShapeDtypeStruct((tok_rows, width), BF16)
    mixed, latent_grad, score_grad = kernel_call(
        functools.partial(combine_body, capacity),
        [row, row, jax.ShapeDtypeStruct((2, tok_rows), F32)],
    )(back, first, second, score_rows, cotangent)
    got, mixed = together((got, mixed))
    lanes = width // 128
    block = jax.ShapeDtypeStruct((hidden_rows * lanes, 128), F32)
    grads = kernel_call(finish_body, [block] * 3)(near_keep, near_got, got)
    grads = [grad.reshape(1, hidden_rows, width) for grad in grads]
    return (mixed, latent_grad, score_grad.T, *grads)


def solution(mesh):
    fine = Mesh(
        mesh.devices.reshape(8, 2, 2, 4, 4), ("z", "yh", "core", "x", "yl")
    )
    fsdp, expert = ("z", "yh", "core"), ("x", "yl")
    rows = P(fsdp + expert, None)
    weight = P(expert, fsdp, None)
    return jax.shard_map(
        shards,
        mesh=fine,
        in_specs=(rows,) * 4 + (weight,) * 3,
        out_specs=(rows,) * 3 + (weight,) * 3,
        check_vma=False,
    )
```

```python
import functools

import jax
import jax.numpy as jnp
from jax import lax
from jax.experimental import pallas as pl
from jax.experimental.pallas import tpu as pltpu
from jax.sharding import Mesh, PartitionSpec as P

grad_scale = 0.015625
PAD = 48
F32 = jnp.float32
BF16 = jnp.bfloat16


def swap_z(rows, parity):
    size = lax.axis_size("z")
    pairs = [(z, (z + (1 if (z + parity) % 2 == 0 else -1)) % size) for z in range(size)]
    return lax.ppermute(rows, "z", pairs)


def swap(rows, axis):
    return lax.ppermute(rows, axis, [(0, 1), (1, 0)])


def add(one, two):
    return one.astype(F32) + two.astype(F32)


together = lax.optimization_barrier


def sum_z(pieces, parity):
    first, second, third, last = pieces
    third = add(third, swap_z(last, parity + 3)).astype(BF16)
    second = add(second, swap_z(third, parity + 2)).astype(BF16)
    first = add(first, swap_z(second, parity + 1))
    return add(first[:1], swap_z(first[1:].astype(BF16), parity))


def dot(left, right, contract):
    return lax.dot_general(left, right, ((contract[:1], contract[1:]), ((), ())), preferred_element_type=F32)


def kernel_call(body, outs, scratch=(), flops=0, grant=24):
    return pl.pallas_call(
        body,
        out_shape=outs,
        scratch_shapes=list(scratch),
        compiler_params=pltpu.CompilerParams(vmem_limit_bytes=grant * 2**20),
        cost_estimate=pl.CostEstimate(flops=flops, bytes_accessed=1 << 20, transcendentals=0),
    )


def dispatch_body(capacity, latent, cotangent, routes, scores, send, first, second):
    experts = send.shape[0]
    slots, rows = first.shape
    width = latent.shape[1]
    slot = lax.broadcasted_iota(jnp.int32, (slots, rows), 0)
    bits = capacity.bit_length() - 1
    expert = slot >> bits
    place = slot & (capacity - 1)
    named_0 = routes[0:1, :] == expert
    named_1 = routes[1:2, :] == expert
    named = jnp.where(named_0 | named_1, 1.0, 0.0)
    upper = lax.broadcasted_iota(jnp.int32, (rows, rows), 0) < lax.broadcasted_iota(
        jnp.int32, (rows, rows), 1
    )
    ranks = dot(named.astype(BF16), jnp.where(upper, 1.0, 0.0).astype(BF16), (1, 0))
    hit = ranks == place.astype(F32)
    one = jnp.where(named_0 & hit, 1.0, 0.0)
    two = jnp.where(named_1 & hit, 1.0, 0.0)
    first[...] = one.astype(BF16)
    second[...] = two.astype(BF16)
    table = (one + two).astype(BF16)
    score = jnp.sum(one * scores[0:1, :] + two * scores[1:2, :], axis=1, keepdims=True)
    placed = dot(table, latent[...], (1, 0)).astype(BF16)
    weighted = (score * dot(table, cotangent[...], (1, 0))).astype(BF16)
    send[:, :capacity, :] = placed.reshape(experts, capacity, width)
    send[:, capacity:, :] = weighted.reshape(experts, capacity, width)


def combine_body(capacity, back, first, second, scores, cotangent, mixed, latent_grad, score_grad):
    slots, rows = first.shape
    width = back.shape[2]
    outs = back[:, :capacity, :].reshape(slots, width)
    tokens = back[:, capacity:, :].reshape(slots, width)
    cot = cotangent[...].astype(F32)
    total = jnp.zeros((rows, width), F32)
    sums = []
    for k, table in enumerate((first, second)):
        picked = dot(table[...], outs, (0, 0))
        score = jnp.broadcast_to(scores[k : k + 1, :], (rows, rows)).T
        total = total + score[:, 0:1] * picked
        own = jnp.sum(cot * picked, axis=1, keepdims=True)
        sums.append(jnp.broadcast_to(own, (rows, rows)).T[0:1, :])
    mixed[...] = total.astype(BF16)
    score_grad[...] = jnp.concatenate(sums, axis=0)
    merged = first[...] + second[...]
    latent_grad[...] = dot(merged, tokens, (0, 0)).astype(BF16)


def expert_body(capacity, count, more, *refs):
    mine, theirs = refs[:2]
    pieces = refs[2 : 2 + count]
    refs = refs[2 + count :]
    if more:
        sums, refs = refs[:2], refs[2:]
    grads = refs[:count]
    results = refs[count : count + 2]
    wg, wu, wd, xs, gs, hs, gbs, ubs = refs[count + 2 :]
    width = mine.shape[2]
    own_rows = pieces[0].shape[1] // 3
    for i, piece in enumerate(pieces):
        for j in range(2):
            start = (2 * i + j) * PAD
            for k, weight in enumerate((wg, wu, wd)):
                weight[start : start + own_rows, :] = piece[j, k * own_rows : (k + 1) * own_rows, :]
                weight[start + own_rows : start + PAD, :] = jnp.zeros((PAD - own_rows, width), BF16)
    sources = mine.shape[0] // 2
    tile = sources * capacity
    for i in range(4):
        tokens = (mine, theirs)[i // 2]
        part = slice((i % 2) * sources, (i % 2 + 1) * sources)
        rows = slice(i * tile, (i + 1) * tile)
        x = tokens[part, :capacity, :].reshape(tile, width)
        g = tokens[part, capacity:, :].reshape(tile, width)
        xs[rows, :] = x
        gs[rows, :] = g
        gate = dot(x, wg[...], (1, 1))
        up = dot(x, wu[...], (1, 1))
        hidden_grad = dot(g, wd[...], (1, 1))
        sig = jax.nn.sigmoid(gate)
        act = gate * sig
        hidden = (act * up).astype(BF16)
        gate_back = (hidden_grad * up * (sig * (1.0 + gate * (1.0 - sig)))).astype(BF16)
        up_back = (hidden_grad * act).astype(BF16)
        hs[rows, :] = hidden
        gbs[rows, :] = gate_back
        ubs[rows, :] = up_back
        outs = dot(hidden, wd[...], (1, 0)).reshape(sources, capacity, width)
        back = dot(gate_back, wg[...], (1, 0)) + dot(up_back, wu[...], (1, 0))
        back = back.reshape(sources, capacity, width)
        result = results[i // 2]
        if more:
            outs = outs + sums[i // 2][part, :capacity, :]
            back = back + sums[i // 2][part, capacity:, :]
        result[part, :capacity, :] = outs.astype(result.dtype)
        result[part, capacity:, :] = back.astype(result.dtype)
    for k, (left, right) in enumerate(((gbs, xs), (ubs, xs), (hs, gs))):
        term = (dot(left[...], right[...], (0, 0)) * grad_scale).astype(BF16)
        for i, grad in enumerate(grads):
            for j in range(2):
                start = (2 * i + j) * PAD
                grad[j, k * own_rows : (k + 1) * own_rows, :] = term[start : start + own_rows, :]


def expert_call(capacity, mine, theirs, pieces, sums=(), last=False):
    both = mine.shape
    width = both[2]
    slots = both[0] * capacity * 2
    count = len(pieces)
    hidden = 2 * count * PAD
    outs = [jax.ShapeDtypeStruct(p.shape, BF16) for p in pieces]
    outs += [jax.ShapeDtypeStruct(both, F32), jax.ShapeDtypeStruct(both, BF16 if last else F32)]
    scratch = [pltpu.VMEM((hidden, width), BF16)] * 3 + [pltpu.VMEM((slots, width), BF16)] * 2
    scratch += [pltpu.VMEM((slots, hidden), BF16)] * 3
    body = functools.partial(expert_body, capacity, count, len(sums) > 0)
    call = kernel_call(body, outs, scratch, 18 * slots * hidden * width)
    got = call(mine, theirs, *pieces, *sums)
    return got[:count], got[count:]


def pair_body(one, two, out):
    out[0:1] = one[...]
    out[1:2] = two[...]


def pair(one, two, flops=0):
    out = jax.ShapeDtypeStruct((2,) + one.shape[1:], one.dtype)
    return kernel_call(pair_body, out, flops=flops, grant=16)(one, two)


def total_body(one, two, out):
    out[...] = (one[...].astype(F32) + two[...].astype(F32)).astype(out.dtype)


def total(one, two, dtype, flops=0):
    out = jax.ShapeDtypeStruct(one.shape, dtype)
    return kernel_call(total_body, out, flops=flops, grant=16)(one, two)


def split_body(one, two, keep, send):
    value = one[...].astype(F32) + two[...].astype(F32)
    keep[...] = value[0:1]
    send[...] = value[1:2].astype(send.dtype)


def split(one, two, flops=0):
    shape = (1,) + one.shape[1:]
    outs = [jax.ShapeDtypeStruct(shape, F32), jax.ShapeDtypeStruct(shape, BF16)]
    return kernel_call(split_body, outs, flops=flops, grant=16)(one, two)


def finish_body(near, near_far, far, *outs):
    value = near[0] + near_far[0].astype(F32) + far[0].astype(F32)
    rows = value.shape[0] // 3
    for k, out in enumerate(outs):
        for j in range(value.shape[1] // 128):
            out[pl.ds(j, rows, stride=value.shape[1] // 128), :] = value[
                k * rows : (k + 1) * rows, j * 128 : (j + 1) * 128
            ]


def shards(latent, routes, scores, cotangent, w_gate, w_up, w_down):
    experts = lax.axis_size("x") * lax.axis_size("yl")
    tok_rows, width = latent.shape
    capacity = 4 * tok_rows // experts
    slots = experts * capacity
    hidden_rows = w_gate.shape[1]
    own = jnp.concatenate([w_gate[0], w_up[0], w_down[0]], axis=0)[None]
    other = swap(own, "yh")

    near_got = swap_z(own, 0)
    shape = (experts, 2 * capacity, width)
    table = jax.ShapeDtypeStruct((slots, tok_rows), BF16)
    score_rows = scores.T
    send, first, second = kernel_call(
        functools.partial(dispatch_body, capacity),
        [jax.ShapeDtypeStruct(shape, BF16), table, table],
        grant=56,
    )(latent, cotangent, routes.T, score_rows)

    other, near_got, send = together((other, near_got, send))
    mine = lax.all_to_all(send, ("x", "yl"), 0, 0, tiled=True)
    near = [jnp.concatenate([own, near_got], axis=0)]
    far_got = swap_z(other, 0)
    near.append(swap_z(near[0], 1))
    far = [pair(other, far_got, 4 * 10**10)]
    near.append(swap_z(near[1], 0))
    far.append(swap_z(far[0], 1))
    near.append(swap_z(near[2], 1))
    far.append(swap_z(far[1], 0))
    near[3], far[2], mine = together((near[3], far[2], mine))
    theirs = swap(mine, "core")
    far.append(swap_z(far[2], 1))

    near_terms, sums = expert_call(capacity, mine, theirs, near)
    early, sums = expert_call(capacity, mine, theirs, far[:3], sums)
    late, (local, rest) = expert_call(capacity, mine, theirs, far[3:], sums, True)
    far_terms = (*early, *late)

    rest = swap(rest, "core")
    got = swap_z(far_terms[3], 1)
    far_sum = total(far_terms[2], got, BF16, 4 * 10**10)
    far_sum, rest = together((far_sum, rest))
    back = lax.all_to_all(add(local, rest).astype(BF16), ("x", "yl"), 0, 0, tiled=True)
    got, near_got = together((swap_z(far_sum, 0), swap_z(near_terms[3], 1)))
    far_sum = total(far_terms[1], got, BF16, 0)
    far_sum, near_got = together((far_sum, near_got))
    near_sum = total(near_terms[2], near_got, BF16, 4 * 10**9)
    got, near_got = together((swap_z(far_sum, 1), swap_z(near_sum, 0)))
    far_keep, far_send = split(far_terms[0], got)
    far_send, near_got = together((far_send, near_got))
    near_sum = total(near_terms[1], near_got, BF16, 4 * 10**9)
    got, near_got = together((swap_z(far_send, 0), swap_z(near_sum, 1)))
    far_sum = total(far_keep, got, BF16)
    far_sum, near_got = together((far_sum, near_got))
    near_keep, near_send = split(near_terms[0], near_got, 4 * 10**9)
    near_got = swap_z(near_send, 0)
    got = swap(far_sum, "yh")
    row = jax.ShapeDtypeStruct((tok_rows, width), BF16)
    mixed, latent_grad, score_grad = kernel_call(
        functools.partial(combine_body, capacity),
        [row, row, jax.ShapeDtypeStruct((2, tok_rows), F32)],
    )(back, first, second, score_rows, cotangent)
    got, mixed = together((got, mixed))
    lanes = width // 128
    block = jax.ShapeDtypeStruct((hidden_rows * lanes, 128), F32)
    grads = kernel_call(finish_body, [block] * 3)(near_keep, near_got, got)
    grads = [grad.reshape(1, hidden_rows, width) for grad in grads]
    return (mixed, latent_grad, score_grad.T, *grads)


def solution(mesh):
    fine = Mesh(
        mesh.devices.reshape(8, 2, 2, 4, 4), ("z", "yh", "core", "x", "yl")
    )
    fsdp, expert = ("z", "yh", "core"), ("x", "yl")
    rows = P(fsdp + expert, None)
    weight = P(expert, fsdp, None)
    return jax.shard_map(
        shards,
        mesh=fine,
        in_specs=(rows,) * 4 + (weight,) * 3,
        out_specs=(rows,) * 3 + (weight,) * 3,
        check_vma=False,
    )
```

```python
import functools

import jax
import jax.numpy as jnp
from jax import lax
from jax.experimental import pallas as pl
from jax.experimental.pallas import tpu as pltpu
from jax.sharding import Mesh, PartitionSpec as P

grad_scale = 0.015625
PAD = 48
F32 = jnp.float32
BF16 = jnp.bfloat16


def swap_z(rows, parity):
    size = lax.axis_size("z")
    pairs = [(z, (z + (1 if (z + parity) % 2 == 0 else -1)) % size) for z in range(size)]
    return lax.ppermute(rows, "z", pairs)


def swap(rows, axis):
    return lax.ppermute(rows, axis, [(0, 1), (1, 0)])


def add(one, two):
    return one.astype(F32) + two.astype(F32)


together = lax.optimization_barrier


def sum_z(pieces, parity):
    first, second, third, last = pieces
    third = add(third, swap_z(last, parity + 3)).astype(BF16)
    second = add(second, swap_z(third, parity + 2)).astype(BF16)
    first = add(first, swap_z(second, parity + 1))
    return add(first[:1], swap_z(first[1:].astype(BF16), parity))


def dot(left, right, contract):
    return lax.dot_general(left, right, ((contract[:1], contract[1:]), ((), ())), preferred_element_type=F32)


def kernel_call(body, outs, scratch=(), flops=0, grant=24):
    return pl.pallas_call(
        body,
        out_shape=outs,
        scratch_shapes=list(scratch),
        compiler_params=pltpu.CompilerParams(vmem_limit_bytes=grant * 2**20),
        cost_estimate=pl.CostEstimate(flops=flops, bytes_accessed=1 << 20, transcendentals=0),
    )


def dispatch_body(capacity, latent, cotangent, routes, scores, send, first, second):
    experts = send.shape[0]
    slots, rows = first.shape
    width = latent.shape[1]
    slot = lax.broadcasted_iota(jnp.int32, (slots, rows), 0)
    bits = capacity.bit_length() - 1
    expert = slot >> bits
    place = slot & (capacity - 1)
    named_0 = routes[0:1, :] == expert
    named_1 = routes[1:2, :] == expert
    named = jnp.where(named_0 | named_1, 1.0, 0.0)
    upper = lax.broadcasted_iota(jnp.int32, (rows, rows), 0) < lax.broadcasted_iota(
        jnp.int32, (rows, rows), 1
    )
    ranks = dot(named.astype(BF16), jnp.where(upper, 1.0, 0.0).astype(BF16), (1, 0))
    hit = ranks == place.astype(F32)
    one = jnp.where(named_0 & hit, 1.0, 0.0)
    two = jnp.where(named_1 & hit, 1.0, 0.0)
    first[...] = one.astype(BF16)
    second[...] = two.astype(BF16)
    table = (one + two).astype(BF16)
    score = jnp.sum(one * scores[0:1, :] + two * scores[1:2, :], axis=1, keepdims=True)
    placed = dot(table, latent[...], (1, 0)).astype(BF16)
    weighted = (score * dot(table, cotangent[...], (1, 0))).astype(BF16)
    send[:, :capacity, :] = placed.reshape(experts, capacity, width)
    send[:, capacity:, :] = weighted.reshape(experts, capacity, width)


def combine_body(capacity, back, first, second, scores, cotangent, mixed, latent_grad, score_grad):
    slots, rows = first.shape
    width = back.shape[2]
    outs = back[:, :capacity, :].reshape(slots, width)
    tokens = back[:, capacity:, :].reshape(slots, width)
    cot = cotangent[...].astype(F32)
    total = jnp.zeros((rows, width), F32)
    sums = []
    for k, table in enumerate((first, second)):
        picked = dot(table[...], outs, (0, 0))
        score = jnp.broadcast_to(scores[k : k + 1, :], (rows, rows)).T
        total = total + score[:, 0:1] * picked
        own = jnp.sum(cot * picked, axis=1, keepdims=True)
        sums.append(jnp.broadcast_to(own, (rows, rows)).T[0:1, :])
    mixed[...] = total.astype(BF16)
    score_grad[...] = jnp.concatenate(sums, axis=0)
    merged = first[...] + second[...]
    latent_grad[...] = dot(merged, tokens, (0, 0)).astype(BF16)


def expert_body(capacity, count, more, *refs):
    mine, theirs = refs[:2]
    pieces = refs[2 : 2 + count]
    refs = refs[2 + count :]
    if more:
        sums, refs = refs[:2], refs[2:]
    grads = refs[:count]
    results = refs[count : count + 2]
    wg, wu, wd, xs, gs, hs, gbs, ubs = refs[count + 2 :]
    width = mine.shape[2]
    own_rows = pieces[0].shape[1] // 3
    for i, piece in enumerate(pieces):
        for j in range(2):
            start = (2 * i + j) * PAD
            for k, weight in enumerate((wg, wu, wd)):
                weight[start : start + own_rows, :] = piece[j, k * own_rows : (k + 1) * own_rows, :]
                weight[start + own_rows : start + PAD, :] = jnp.zeros((PAD - own_rows, width), BF16)
    sources = mine.shape[0] // 2
    tile = sources * capacity
    for i in range(4):
        tokens = (mine, theirs)[i // 2]
        part = slice((i % 2) * sources, (i % 2 + 1) * sources)
        rows = slice(i * tile, (i + 1) * tile)
        x = tokens[part, :capacity, :].reshape(tile, width)
        g = tokens[part, capacity:, :].reshape(tile, width)
        xs[rows, :] = x
        gs[rows, :] = g
        gate = dot(x, wg[...], (1, 1))
        up = dot(x, wu[...], (1, 1))
        hidden_grad = dot(g, wd[...], (1, 1))
        sig = jax.nn.sigmoid(gate)
        act = gate * sig
        hidden = (act * up).astype(BF16)
        gate_back = (hidden_grad * up * (sig * (1.0 + gate * (1.0 - sig)))).astype(BF16)
        up_back = (hidden_grad * act).astype(BF16)
        hs[rows, :] = hidden
        gbs[rows, :] = gate_back
        ubs[rows, :] = up_back
        outs = dot(hidden, wd[...], (1, 0)).reshape(sources, capacity, width)
        back = dot(gate_back, wg[...], (1, 0)) + dot(up_back, wu[...], (1, 0))
        back = back.reshape(sources, capacity, width)
        result = results[i // 2]
        if more:
            outs = outs + sums[i // 2][part, :capacity, :]
            back = back + sums[i // 2][part, capacity:, :]
        result[part, :capacity, :] = outs.astype(result.dtype)
        result[part, capacity:, :] = back.astype(result.dtype)
    for k, (left, right) in enumerate(((gbs, xs), (ubs, xs), (hs, gs))):
        term = (dot(left[...], right[...], (0, 0)) * grad_scale).astype(BF16)
        for i, grad in enumerate(grads):
            for j in range(2):
                start = (2 * i + j) * PAD
                grad[j, k * own_rows : (k + 1) * own_rows, :] = term[start : start + own_rows, :]


def expert_call(capacity, mine, theirs, pieces, sums=(), last=False):
    both = mine.shape
    width = both[2]
    slots = both[0] * capacity * 2
    count = len(pieces)
    hidden = 2 * count * PAD
    outs = [jax.ShapeDtypeStruct(p.shape, BF16) for p in pieces]
    outs += [jax.ShapeDtypeStruct(both, F32), jax.ShapeDtypeStruct(both, BF16 if last else F32)]
    scratch = [pltpu.VMEM((hidden, width), BF16)] * 3 + [pltpu.VMEM((slots, width), BF16)] * 2
    scratch += [pltpu.VMEM((slots, hidden), BF16)] * 3
    body = functools.partial(expert_body, capacity, count, len(sums) > 0)
    call = kernel_call(body, outs, scratch, 18 * slots * hidden * width)
    got = call(mine, theirs, *pieces, *sums)
    return got[:count], got[count:]


def pair_body(one, two, out):
    out[0:1] = one[...]
    out[1:2] = two[...]


def pair(one, two, flops=0):
    out = jax.ShapeDtypeStruct((2,) + one.shape[1:], one.dtype)
    return kernel_call(pair_body, out, flops=flops, grant=16)(one, two)


def total_body(one, two, out):
    out[...] = (one[...].astype(F32) + two[...].astype(F32)).astype(out.dtype)


def total(one, two, dtype, flops=0):
    out = jax.ShapeDtypeStruct(one.shape, dtype)
    return kernel_call(total_body, out, flops=flops, grant=16)(one, two)


def split_body(one, two, keep, send):
    value = one[...].astype(F32) + two[...].astype(F32)
    keep[...] = value[0:1]
    send[...] = value[1:2].astype(send.dtype)


def split(one, two, flops=0):
    shape = (1,) + one.shape[1:]
    outs = [jax.ShapeDtypeStruct(shape, F32), jax.ShapeDtypeStruct(shape, BF16)]
    return kernel_call(split_body, outs, flops=flops, grant=16)(one, two)


def finish_body(near, near_far, far, *outs):
    value = near[0] + near_far[0].astype(F32) + far[0].astype(F32)
    rows = value.shape[0] // 3
    for k, out in enumerate(outs):
        for j in range(value.shape[1] // 128):
            out[pl.ds(j, rows, stride=value.shape[1] // 128), :] = value[
                k * rows : (k + 1) * rows, j * 128 : (j + 1) * 128
            ]


def shards(latent, routes, scores, cotangent, w_gate, w_up, w_down):
    experts = lax.axis_size("x") * lax.axis_size("yl")
    tok_rows, width = latent.shape
    capacity = 4 * tok_rows // experts
    slots = experts * capacity
    hidden_rows = w_gate.shape[1]
    own = jnp.concatenate([w_gate[0], w_up[0], w_down[0]], axis=0)[None]
    other = swap(own, "yh")

    near_got = swap_z(own, 0)
    shape = (experts, 2 * capacity, width)
    table = jax.ShapeDtypeStruct((slots, tok_rows), BF16)
    score_rows = scores.T
    send, first, second = kernel_call(
        functools.partial(dispatch_body, capacity),
        [jax.ShapeDtypeStruct(shape, BF16), table, table],
        grant=56,
    )(latent, cotangent, routes.T, score_rows)

    other, near_got, send = together((other, near_got, send))
    mine = lax.all_to_all(send, ("x", "yl"), 0, 0, tiled=True)
    near = [jnp.concatenate([own, near_got], axis=0)]
    far_got = swap_z(other, 0)
    near.append(swap_z(near[0], 1))
    far = [pair(other, far_got, 4 * 10**10)]
    near.append(swap_z(near[1], 0))
    far.append(swap_z(far[0], 1))
    near.append(swap_z(near[2], 1))
    far.append(swap_z(far[1], 0))
    near[3], far[2], mine = together((near[3], far[2], mine))
    theirs = swap(mine, "core")
    far.append(swap_z(far[2], 1))

    near_terms, sums = expert_call(capacity, mine, theirs, near)
    early, sums = expert_call(capacity, mine, theirs, far[:3], sums)
    late, (local, rest) = expert_call(capacity, mine, theirs, far[3:], sums, True)
    far_terms = (*early, *late)

    rest = swap(rest, "core")
    got = swap_z(far_terms[3], 1)
    far_sum = total(far_terms[2], got, BF16, 4 * 10**10)
    far_sum, rest = together((far_sum, rest))
    back = lax.all_to_all(add(local, rest).astype(BF16), ("x", "yl"), 0, 0, tiled=True)
    got, near_got = together((swap_z(far_sum, 0), swap_z(near_terms[3], 1)))
    far_sum = total(far_terms[1], got, BF16, 0)
    far_sum, near_got = together((far_sum, near_got))
    near_sum = total(near_terms[2], near_got, BF16, 4 * 10**9)
    got, near_got = swap_z(far_sum, 1), swap_z(near_sum, 0)
    far_keep, far_send = split(far_terms[0], got)
    near_sum = total(near_terms[1], near_got, BF16, 4 * 10**9)
    got, near_got = swap_z(far_send, 0), swap_z(near_sum, 1)
    far_sum = total(far_keep, got, BF16)
    near_keep, near_send = split(near_terms[0], near_got, 4 * 10**9)
    near_got = swap_z(near_send, 0)
    got = swap(far_sum, "yh")
    row = jax.ShapeDtypeStruct((tok_rows, width), BF16)
    mixed, latent_grad, score_grad = kernel_call(
        functools.partial(combine_body, capacity),
        [row, row, jax.ShapeDtypeStruct((2, tok_rows), F32)],
    )(back, first, second, score_rows, cotangent)
    got, mixed = together((got, mixed))
    lanes = width // 128
    block = jax.ShapeDtypeStruct((hidden_rows * lanes, 128), F32)
    grads = kernel_call(finish_body, [block] * 3)(near_keep, near_got, got)
    grads = [grad.reshape(1, hidden_rows, width) for grad in grads]
    return (mixed, latent_grad, score_grad.T, *grads)


def solution(mesh):
    fine = Mesh(
        mesh.devices.reshape(8, 2, 2, 4, 4), ("z", "yh", "core", "x", "yl")
    )
    fsdp, expert = ("z", "yh", "core"), ("x", "yl")
    rows = P(fsdp + expert, None)
    weight = P(expert, fsdp, None)
    return jax.shard_map(
        shards,
        mesh=fine,
        in_specs=(rows,) * 4 + (weight,) * 3,
        out_specs=(rows,) * 3 + (weight,) * 3,
        check_vma=False,
    )
```
